32 devices in a mesh: parts: 2 (over x), rows: 16 (over z, y, core).
Axes of the slice: x: 2, y: 2, z: 4, core: 2. Of those that a mesh axis runs over, the one named last changes fastest.
Arguments:
- traces: bfloat16 [16, 4096, 2048], P('parts', 'rows'), parts along dimension 0, may hold values from -6 to 6
- offset_bin: int32 [16, 4096], P('parts', 'rows'), parts along dimension 0, may hold values from 0 to 15
- filters: float32 [16, 32], replicated, may hold values from -1 to 1
- data_matrix: bfloat16 [128, 2, 64, 4096], P('parts', None, 'rows'), parts along dimension 0, may hold values from -0.0625 to 0.0625
Outputs:
- multiples: bfloat16 [128, 2, 8, 64], P(('parts', 'rows')), parts along dimension 0
The draws below stay inside these ranges and needn't reach their ends.
There are 2 independent parts, one for each index of `parts`. The reference program is written for one: setup_inputs(seed, part) draws one part's arguments, and reference() takes and returns one part's arrays. A program takes and returns all parts, laid end to end along the dimension named above; an argument that names none is the same for every part. Nothing has to cross between parts.
All inputs are finite; a program needn't handle non-finite values.
Results may differ from the reference program's by a relative error of at most 0.0067.
Values may be sent and summed in bfloat16 or wider, within the bound.
A program may use at most 128 MiB of HBM per device.

```python
import math
import jax
import jax.numpy as jnp
from jax import lax

NR = 4096
NT = 2048
NF = 64
FIRST = 64
TAPS = 32
BINS = 16
SHOTS = 8
RW = 64


def set_ends(entries, key, low, high):
    dims = entries.shape
    place = [jax.random.randint(jax.random.fold_in(key, axis), (), 0, dims[axis]) for axis in range(len(dims))]
    entries = entries.at[tuple(place)].set(low)
    longest = dims.index(max(dims))
    place[longest] = (place[longest] + 1) % dims[longest]
    return entries.at[tuple(place)].set(high)


def block_levels(key, dims, pieces, smallest, high):
    def one(position, shards_of):
        draws = jax.random.uniform(jax.random.fold_in(jax.random.fold_in(key, 6), position), (shards_of,), jnp.float32, smallest / len(pieces), high / len(pieces))
        return jnp.repeat(jnp.exp(draws), dims[position] // shards_of).reshape((-1,) + (1,) * (len(dims) - position - 1))

    loudness = one(*pieces[0])
    for cut in pieces[1:]:
        loudness = loudness * one(*cut)
    return loudness


def scatter_about(own_key, shape, scale, limit, pieces=(), kind=jnp.bfloat16):
    array = jax.random.normal(own_key, shape, jnp.float32) * scale
    if len(pieces) > 0:
        array = block_levels(own_key, shape, pieces, -0.22, 0.18) * array
    return jnp.clip(array, min=-limit, max=limit).astype(kind)


def setup_inputs(seed: int = 0, part: int = 0) -> dict:
    keys = jax.random.split(jax.random.key(seed), 5)
    part_keys = jax.random.split(jax.random.fold_in(keys[4], part), 5)
    traces = scatter_about(part_keys[0], (SHOTS, NR, NT), 1.0, 6.0, ((1, 16),))
    offset_bin = set_ends(jax.random.randint(part_keys[1], (SHOTS, NR), 0, BINS), jax.random.fold_in(part_keys[1], 1), 0, BINS - 1).astype(jnp.int32)
    filters = scatter_about(keys[2], (BINS, TAPS), TAPS ** -0.5, 1.0, (), jnp.float32)
    data_matrix = scatter_about(part_keys[3], (NF, 2, RW, NR), (2 * NR) ** -0.5, 0.0625, ((2, 16),))
    return {"traces": traces, "offset_bin": offset_bin, "filters": filters, "data_matrix": data_matrix}


def spectral_table(freq_count, first_index, length):
    freq_index = first_index + jnp.arange(freq_count, dtype=jnp.int32)
    sample_index = jnp.arange(length, dtype=jnp.int32)
    product_index = freq_index[:, None] * sample_index[None, :] % length
    phase_angle = product_index.astype(jnp.float32) * jnp.float32(2.0 * math.pi / length)
    norm_factor = jnp.float32(1.0 / math.sqrt(length))
    stacked = jnp.stack([jnp.cos(phase_angle), -jnp.sin(phase_angle)], axis=1) * norm_factor
    return stacked.astype(jnp.bfloat16)

def reference(traces, offset_bin, filters, data_matrix):
    table = spectral_table(NF, FIRST, NT).reshape(2 * NF, NT)

    def one_shot(inputs):
        shot_traces, shot_bins = inputs
        tap_rows = filters[shot_bins]
        padded = jnp.pad(shot_traces, ((0, 0), (TAPS - 1, 0)))
        filtered = jnp.zeros((NR, NT), jnp.float32)
        for delay_index in range(TAPS):
            window = padded[:, TAPS - 1 - delay_index:TAPS - 1 - delay_index + NT]
            filtered = filtered + tap_rows[:, delay_index:delay_index + 1] * window.astype(jnp.float32)
        filtered = filtered.astype(jnp.bfloat16)
        return jnp.dot(table, filtered.T, preferred_element_type=jnp.float32).astype(jnp.bfloat16)
    spectra = lax.map(one_shot, (traces, offset_bin))
    spectra = jnp.transpose(spectra.reshape(SHOTS, NF, 2, NR), (1, 2, 0, 3))

    def one_freq(inputs):
        matrix_rows, shot_columns = inputs
        matrix_rows = matrix_rows.astype(jnp.float32)
        shot_columns = shot_columns.astype(jnp.float32)
        highest = lax.Precision.HIGHEST
        real_part = jnp.einsum('rk,sk->sr', matrix_rows[0], shot_columns[0], precision=highest) - jnp.einsum('rk,sk->sr', matrix_rows[1], shot_columns[1], precision=highest)
        imag_part = jnp.einsum('rk,sk->sr', matrix_rows[0], shot_columns[1], precision=highest) + jnp.einsum('rk,sk->sr', matrix_rows[1], shot_columns[0], precision=highest)
        return jnp.stack([real_part, imag_part]).astype(jnp.bfloat16)
    return lax.map(one_freq, (data_matrix, spectra))
```

```python
import functools
import math

import jax
import jax.numpy as jnp
import ml_dtypes
import numpy as np
from jax import lax
from jax.experimental import pallas as pl
from jax.experimental.pallas import tpu as pltpu
from jax.sharding import PartitionSpec as P

FIRST = 64
GROUP = 16
MESH = pl.DeviceIdType.MESH


def spectral_table(freq_count, first_index, length):
    freq_index = first_index + jnp.arange(freq_count, dtype=jnp.int32)
    sample_index = jnp.arange(length, dtype=jnp.int32)
    product_index = freq_index[:, None] * sample_index[None, :] % length
    phase_angle = product_index.astype(jnp.float32) * jnp.float32(2.0 * math.pi / length)
    norm_factor = jnp.float32(1.0 / math.sqrt(length))
    stacked = jnp.stack([jnp.cos(phase_angle), -jnp.sin(phase_angle)], axis=1) * norm_factor
    return stacked.astype(jnp.bfloat16)


def condition(traces, offset_bin, filters):
    bin_count, tap_count = filters.shape
    length = traces.shape[2]
    selector = (
        offset_bin[:, :, None] == jnp.arange(bin_count, dtype=jnp.int32)[None, None, :]
    ).astype(jnp.float32)
    tap_rows = jnp.einsum("skb,bj->skj", selector, filters, precision=lax.Precision.HIGHEST)
    padded = jnp.pad(traces, ((0, 0), (0, 0), (tap_count - 1, 0)))
    filtered = jnp.zeros(traces.shape, jnp.float32)
    for delay_index in range(tap_count):
        window = padded[:, :, tap_count - 1 - delay_index : tap_count - 1 - delay_index + length]
        filtered = filtered + tap_rows[:, :, delay_index : delay_index + 1] * window.astype(
            jnp.float32
        )
    return filtered.astype(jnp.bfloat16)


def spectra_of(filtered, table):
    shot_count, receivers, length = filtered.shape
    flat_table = table.reshape(-1, length)
    flat_signal = filtered.reshape(shot_count * receivers, length)
    values = lax.dot_general(
        flat_table, flat_signal, (((1,), (1,)), ((), ())), preferred_element_type=jnp.float32
    )
    return values.astype(jnp.bfloat16).reshape(table.shape[0], 2, shot_count * receivers)


def predict(matrix_block, spectral_block):
    real_part = jnp.einsum(
        "tion,toun->tui",
        matrix_block[:, 0],
        spectral_block[:, 0],
        preferred_element_type=jnp.float32,
    ) - jnp.einsum(
        "tion,toun->tui",
        matrix_block[:, 1],
        spectral_block[:, 1],
        preferred_element_type=jnp.float32,
    )
    imag_part = jnp.einsum(
        "tion,toun->tui",
        matrix_block[:, 0],
        spectral_block[:, 1],
        preferred_element_type=jnp.float32,
    ) + jnp.einsum(
        "tion,toun->tui",
        matrix_block[:, 1],
        spectral_block[:, 0],
        preferred_element_type=jnp.float32,
    )
    return jnp.stack([real_part, imag_part], axis=1)


def plain(traces, offset_bin, filters, data_matrix):
    shot_count, receivers, length = traces.shape
    freq_count = data_matrix.shape[0]
    row_count = data_matrix.shape[2]
    table = spectral_table(freq_count, FIRST, length)
    spectra = spectra_of(condition(traces, offset_bin, filters), table)
    tile_width = shot_count * receivers
    gathered = lax.all_gather(spectra, "rows", axis=2, tiled=True)
    groups = gathered.shape[2] // tile_width
    matrix_block = data_matrix.reshape(freq_count, 2, row_count, groups, receivers)
    spectral_block = gathered.reshape(freq_count, 2, groups, shot_count, receivers)
    partial_value = predict(matrix_block, spectral_block)
    return lax.all_to_all(
        partial_value.astype(jnp.bfloat16), "rows", split_axis=0, concat_axis=3, tiled=True
    )


def phases(index, length):
    angle = (index % length).astype(np.float64) * (2.0 * math.pi / length)
    return np.cos(angle), -np.sin(angle)


def constants(freq_count, length, taps, bins):
    freq = FIRST + np.arange(freq_count, dtype=np.int64)
    norm = 1.0 / math.sqrt(length)
    head = np.stack(phases(freq[:, None] * np.arange(length)[None], length)) * norm
    head[:, :, length - taps :] = 0.0
    head = head.reshape(2 * freq_count, length).astype(np.float32).astype(ml_dtypes.bfloat16)
    lag = np.stack(phases(freq[:, None] * np.arange(taps)[None], length))
    lag = lag.reshape(2 * freq_count, taps).astype(np.float32)
    last = np.stack(phases(freq[:, None] * (length - taps + np.arange(taps))[None], length)) * norm
    last = np.tile(last, (1, 1, bins)).astype(np.float32)
    return head, lag, last


def fused_kernel(
    dims, traces_hbm, bins_ref, filters_ref, cut_ref, head_ref, lag_ref, last_ref, matrix_hbm,
    out_ref,
    traces_buf, spectra, matrix_buf, total, tail_ref, folded, partials, landed,
    trace_sem, own_sem, pair_send, pair_recv,
    right_send, right_recv, left_send, left_recv, out_send, out_recv,
):
    n, shots, receivers, length, freqs, taps, bin_count, rows = dims
    chips, half = n // 2, n // 4
    groups = freqs // GROUP
    width = GROUP * 2 * rows
    me = lax.axis_index("rows")
    chip, core = me // 2, me % 2
    place = jnp.where(chip % 2 == 0, chip // 2, chips - 1 - chip // 2)

    def chip_at(position):
        position = (position + 2 * chips) % chips
        return jnp.where(position < half, 2 * position, 2 * (chips - 1 - position) + 1)

    right = chip_at(place + 1) * 2 + core
    left = chip_at(place - 1) * 2 + core
    sibling = chip * 2 + 1 - core

    def trace_copy(shot):
        return pltpu.make_async_copy(traces_hbm.at[shot], traces_buf.at[shot], trace_sem.at[shot])

    for shot in range(shots):
        trace_copy(shot).start()

    barrier = pltpu.get_barrier_semaphore()
    for step in range(1, n):
        pl.semaphore_signal(
            barrier, inc=1, device_id={"rows": (me + step) % n}, device_id_type=MESH
        )

    def columns(block, side):
        return pl.ds(pl.multiple_of((block * 2 + side) * receivers, receivers), receivers)

    def lanes():
        return pl.ds(pl.multiple_of(core * width, width), width)

    def own_copy(block):
        return pltpu.make_async_copy(
            matrix_hbm.at[:, :, columns(block, core)],
            matrix_buf.at[block, :, lanes(), :],
            own_sem.at[block],
        )

    def pair_copy(block):
        return pltpu.make_async_remote_copy(
            src_ref=matrix_hbm.at[:, :, columns(block, 1 - core)],
            dst_ref=matrix_buf.at[block, :, lanes(), :],
            send_sem=pair_send.at[block],
            recv_sem=pair_recv.at[block],
            device_id={"rows": sibling},
            device_id_type=MESH,
        )

    def ring_copy(step, shot, rightward):
        block = chip_at(place - (step - 1)) if rightward else chip_at(place + (step - 1))
        send, recv = (right_send, right_recv) if rightward else (left_send, left_recv)
        return pltpu.make_async_remote_copy(
            src_ref=spectra.at[block, shot],
            dst_ref=spectra.at[block, shot],
            send_sem=send.at[step - 1, shot],
            recv_sem=recv.at[step - 1, shot],
            device_id={"rows": right if rightward else left},
            device_id_type=MESH,
        )

    def arrival(step, shot, rightward):
        block = chip_at(place - step) if rightward else chip_at(place + step)
        send, recv = (right_send, right_recv) if rightward else (left_send, left_recv)
        return pltpu.make_async_remote_copy(
            src_ref=spectra.at[block, shot],
            dst_ref=spectra.at[block, shot],
            send_sem=send.at[step - 1, shot],
            recv_sem=recv.at[step - 1, shot],
            device_id={"rows": right if rightward else left},
            device_id_type=MESH,
        )

    def reach(shot, rightward):
        return half if (shot % 2 == 0) == rightward else half - 1

    highest = lax.Precision.HIGHEST
    contract = (((1,), (1,)), ((), ()))
    gains = lax.dot_general(
        lag_ref[...], filters_ref[...], contract, precision=highest,
        preferred_element_type=jnp.float32,
    )
    cut = lax.dot_general(
        lag_ref[...], cut_ref[...], contract, precision=highest,
        preferred_element_type=jnp.float32,
    )
    cut_re, cut_im = cut[:freqs], cut[freqs:]
    last_re, last_im = last_ref[0], last_ref[1]
    tail_ref[:freqs] = (cut_re * last_re - cut_im * last_im).astype(jnp.bfloat16)
    tail_ref[freqs:] = (cut_re * last_im + cut_im * last_re).astype(jnp.bfloat16)
    bin_index = lax.broadcasted_iota(jnp.int32, (bin_count, receivers), 0)

    for shot in range(shots):
        trace_copy(shot).wait()
        chosen = bins_ref[shot : shot + 1, :]
        transform = lax.dot_general(
            head_ref[...], traces_buf[shot], contract, preferred_element_type=jnp.float32
        )
        onehot = (bin_index == chosen).astype(jnp.float32)
        gain = lax.dot_general(
            gains, onehot, (((1,), (0,)), ((), ())), precision=highest,
            preferred_element_type=jnp.float32,
        )
        ending = traces_buf[shot, :, length - 128 :].astype(jnp.float32).T[128 - taps :]
        masked = jnp.concatenate(
            [jnp.where(chosen == b, ending, 0.0) for b in range(bin_count)], axis=0
        ).astype(jnp.bfloat16)
        tail = jnp.dot(tail_ref[...], masked, preferred_element_type=jnp.float32)
        re, im = transform[:freqs], transform[freqs:]
        gain_re, gain_im = gain[:freqs], gain[freqs:]
        spectra[chip, shot, 0] = (re * gain_re - im * gain_im + tail[:freqs]).astype(jnp.bfloat16)
        spectra[chip, shot, 1] = (re * gain_im + im * gain_re + tail[freqs:]).astype(jnp.bfloat16)
        if shot == 0:
            pl.semaphore_wait(barrier, n - 1)
        for rightward in (True, False):
            ring_copy(1, shot, rightward).start()
        if shot == 0:
            for block in range(chips):
                own_copy(block).start()
                pair_copy(block).start()

    def multiply(block, first=False):
        for group in range(groups):
            signal = spectra[block, :, :, group * GROUP : (group + 1) * GROUP, :]
            product = lax.dot_general(
                signal.reshape(shots * 2 * GROUP, receivers), matrix_buf[block, group], contract,
                preferred_element_type=jnp.float32,
            )
            total[group] = product if first else total[group] + product

    for step in range(1, half + 1):
        for shot in range(shots):
            for rightward in (True, False):
                limit = reach(shot, rightward)
                if step <= limit:
                    arrival(step, shot, rightward).wait_recv()
                if step + 1 <= limit:
                    ring_copy(step + 1, shot, rightward).start()
        if step == 1:
            for block in range(chips):
                own_copy(block).wait()
                pair_copy(block).wait_recv()
            multiply(chip, True)
        multiply(chip_at(place - step))
        if step < half:
            multiply(chip_at(place + step))

    lane = lax.broadcasted_iota(jnp.int32, (GROUP, 2 * width), 1)
    diagonal = (lane % width) // (2 * rows) == lax.broadcasted_iota(
        jnp.int32, (GROUP, 2 * width), 0
    )
    for group in range(groups):
        for shot in range(shots):
            for part in range(2):
                start = (shot * 2 + part) * GROUP
                piece = jnp.where(diagonal, total[group, start : start + GROUP, :], 0.0)
                folded[part, shot : shot + 1, :] = jnp.sum(piece, axis=0, keepdims=True)
        straight, crossed = folded[0], folded[1]
        side = lax.broadcasted_iota(jnp.int32, (shots, 2 * width), 1) // rows % 2
        ahead = pltpu.roll(crossed, 2 * width - rows, 1)
        behind = pltpu.roll(crossed, rows, 1)
        partials[group] = jnp.where(side == 0, straight - ahead, straight + behind)

    share = freqs // n

    def out_copy(step):
        target = (me + step) % n
        return pltpu.make_async_remote_copy(
            src_ref=partials.at[target * share // GROUP],
            dst_ref=landed.at[me],
            send_sem=out_send.at[step - 1],
            recv_sem=out_recv.at[step - 1],
            device_id={"rows": target},
            device_id_type=MESH,
        )

    def out_arrival(step):
        source = (me + n - step) % n
        return pltpu.make_async_remote_copy(
            src_ref=partials.at[0],
            dst_ref=landed.at[source],
            send_sem=out_send.at[step - 1],
            recv_sem=out_recv.at[step - 1],
            device_id={"rows": source},
            device_id_type=MESH,
        )

    for step in range(1, n):
        out_copy(step).start()
    landed[me] = partials[me * share // GROUP]
    for step in range(1, n):
        out_arrival(step).wait_recv()
    for block in range(chips):
        out_ref[block] = landed[2 * block] + landed[2 * block + 1]

    for step in range(1, half + 1):
        for shot in range(shots):
            for rightward in (True, False):
                if step <= reach(shot, rightward):
                    ring_copy(step, shot, rightward).wait_send()
    for block in range(chips):
        pair_copy(block).wait_send()
    for step in range(1, n):
        out_copy(step).wait_send()


def fused(n, traces, offset_bin, filters, data_matrix):
    shots, receivers, length = traces.shape
    freqs, _, rows, positions = data_matrix.shape
    bin_count, taps = filters.shape
    chips, half, groups, width = n // 2, n // 4, freqs // GROUP, GROUP * 2 * rows
    head, lag, last = constants(freqs, length, taps, bin_count)
    keep = np.arange(taps)[:, None] + np.arange(taps)[None, :] < taps
    cut = jnp.where(keep[None], filters[:, None, :], 0.0).reshape(bin_count * taps, taps)
    matrix = data_matrix.reshape(groups, width, positions)
    dims = (n, shots, receivers, length, freqs, taps, bin_count, rows)
    vmem = pl.BlockSpec(memory_space=pltpu.VMEM)
    hbm = pl.BlockSpec(memory_space=pl.ANY)
    dma = pltpu.SemaphoreType.DMA
    landed = pl.pallas_call(
        functools.partial(fused_kernel, dims),
        out_shape=jax.ShapeDtypeStruct((chips, shots, 2 * width), jnp.float32),
        in_specs=[hbm, vmem, vmem, vmem, vmem, vmem, vmem, hbm],
        out_specs=vmem,
        scratch_shapes=[
            pltpu.VMEM((shots, receivers, length), jnp.bfloat16),
            pltpu.VMEM((chips, shots, 2, freqs, receivers), jnp.bfloat16),
            pltpu.VMEM((chips, groups, 2 * width, receivers), jnp.bfloat16),
            pltpu.VMEM((groups, shots * 2 * GROUP, 2 * width), jnp.float32),
            pltpu.VMEM((2 * freqs, bin_count * taps), jnp.bfloat16),
            pltpu.VMEM((2, shots, 2 * width), jnp.float32),
            pltpu.VMEM((groups, shots, 2 * width), jnp.float32),
            pltpu.VMEM((n, shots, 2 * width), jnp.float32),
            dma((shots,)), dma((chips,)), dma((chips,)), dma((chips,)),
            dma((half, shots)), dma((half, shots)), dma((half, shots)), dma((half, shots)),
            dma((n - 1,)), dma((n - 1,)),
        ],
        compiler_params=pltpu.CompilerParams(
            collective_id=0, has_side_effects=True, vmem_limit_bytes=60 * 1024 * 1024
        ),
    )(traces, offset_bin, filters, cut, head, lag, last, matrix)
    share = freqs // n
    me = lax.axis_index("rows")
    split = landed.reshape(chips, shots, 2, GROUP, 2, rows)
    mine = lax.dynamic_slice_in_dim(split, me * share % GROUP, share, axis=3)
    ordered = mine.transpose(3, 4, 1, 0, 2, 5)
    return ordered.reshape(share, 2, shots, n * rows).astype(jnp.bfloat16)


def shards(n, traces, offset_bin, filters, data_matrix):
    freqs, _, rows, _ = data_matrix.shape
    share = freqs // n
    fits = (
        n % 4 == 0 and traces.shape[1] % 128 == 0 and traces.shape[2] % 128 == 0
        and freqs % GROUP == 0 and share > 0 and GROUP % share == 0
        and GROUP * 2 * rows % 128 == 0 and filters.shape[1] <= 128
    )
    if fits:
        return fused(n, traces, offset_bin, filters, data_matrix)
    return plain(traces, offset_bin, filters, data_matrix)


def solution(mesh):
    in_specs = (P("parts", "rows", None), P("parts", "rows"), P(), P("parts", None, "rows", None))
    out_specs = P(("parts", "rows"), None, None, None)
    body = functools.partial(shards, mesh.shape["rows"])
    return jax.shard_map(body, mesh=mesh, in_specs=in_specs, out_specs=out_specs, check_vma=False)
```

```python
import functools
import math

import jax
import jax.numpy as jnp
import ml_dtypes
import numpy as np
from jax import lax
from jax.experimental import pallas as pl
from jax.experimental.pallas import tpu as pltpu
from jax.sharding import PartitionSpec as P

FIRST = 64
GROUP = 16
MESH = pl.DeviceIdType.MESH


def spectral_table(freq_count, first_index, length):
    freq_index = first_index + jnp.arange(freq_count, dtype=jnp.int32)
    sample_index = jnp.arange(length, dtype=jnp.int32)
    product_index = freq_index[:, None] * sample_index[None, :] % length
    phase_angle = product_index.astype(jnp.float32) * jnp.float32(2.0 * math.pi / length)
    norm_factor = jnp.float32(1.0 / math.sqrt(length))
    stacked = jnp.stack([jnp.cos(phase_angle), -jnp.sin(phase_angle)], axis=1) * norm_factor
    return stacked.astype(jnp.bfloat16)


def condition(traces, offset_bin, filters):
    bin_count, tap_count = filters.shape
    length = traces.shape[2]
    selector = (
        offset_bin[:, :, None] == jnp.arange(bin_count, dtype=jnp.int32)[None, None, :]
    ).astype(jnp.float32)
    tap_rows = jnp.einsum("skb,bj->skj", selector, filters, precision=lax.Precision.HIGHEST)
    padded = jnp.pad(traces, ((0, 0), (0, 0), (tap_count - 1, 0)))
    filtered = jnp.zeros(traces.shape, jnp.float32)
    for delay_index in range(tap_count):
        window = padded[:, :, tap_count - 1 - delay_index : tap_count - 1 - delay_index + length]
        filtered = filtered + tap_rows[:, :, delay_index : delay_index + 1] * window.astype(
            jnp.float32
        )
    return filtered.astype(jnp.bfloat16)


def spectra_of(filtered, table):
    shot_count, receivers, length = filtered.shape
    flat_table = table.reshape(-1, length)
    flat_signal = filtered.reshape(shot_count * receivers, length)
    values = lax.dot_general(
        flat_table, flat_signal, (((1,), (1,)), ((), ())), preferred_element_type=jnp.float32
    )
    return values.astype(jnp.bfloat16).reshape(table.shape[0], 2, shot_count * receivers)


def predict(matrix_block, spectral_block):
    real_part = jnp.einsum(
        "tion,toun->tui",
        matrix_block[:, 0],
        spectral_block[:, 0],
        preferred_element_type=jnp.float32,
    ) - jnp.einsum(
        "tion,toun->tui",
        matrix_block[:, 1],
        spectral_block[:, 1],
        preferred_element_type=jnp.float32,
    )
    imag_part = jnp.einsum(
        "tion,toun->tui",
        matrix_block[:, 0],
        spectral_block[:, 1],
        preferred_element_type=jnp.float32,
    ) + jnp.einsum(
        "tion,toun->tui",
        matrix_block[:, 1],
        spectral_block[:, 0],
        preferred_element_type=jnp.float32,
    )
    return jnp.stack([real_part, imag_part], axis=1)


def plain(traces, offset_bin, filters, data_matrix):
    shot_count, receivers, length = traces.shape
    freq_count = data_matrix.shape[0]
    row_count = data_matrix.shape[2]
    table = spectral_table(freq_count, FIRST, length)
    spectra = spectra_of(condition(traces, offset_bin, filters), table)
    tile_width = shot_count * receivers
    gathered = lax.all_gather(spectra, "rows", axis=2, tiled=True)
    groups = gathered.shape[2] // tile_width
    matrix_block = data_matrix.reshape(freq_count, 2, row_count, groups, receivers)
    spectral_block = gathered.reshape(freq_count, 2, groups, shot_count, receivers)
    partial_value = predict(matrix_block, spectral_block)
    return lax.all_to_all(
        partial_value.astype(jnp.bfloat16), "rows", split_axis=0, concat_axis=3, tiled=True
    )


def phases(index, length):
    angle = (index % length).astype(np.float64) * (2.0 * math.pi / length)
    return np.cos(angle), -np.sin(angle)


def constants(freq_count, length, taps, bins):
    freq = FIRST + np.arange(freq_count, dtype=np.int64)
    norm = 1.0 / math.sqrt(length)
    head = np.stack(phases(freq[:, None] * np.arange(length)[None], length)) * norm
    head[:, :, length - taps :] = 0.0
    head = head.reshape(2 * freq_count, length).astype(np.float32).astype(ml_dtypes.bfloat16)
    lag = np.stack(phases(freq[:, None] * np.arange(taps)[None], length))
    lag = lag.reshape(2 * freq_count, taps).astype(np.float32)
    last = np.stack(phases(freq[:, None] * (length - taps + np.arange(taps))[None], length)) * norm
    last = np.tile(last, (1, 1, bins)).astype(np.float32)
    return head, lag, last


def fused_kernel(
    dims, traces_hbm, bins_ref, filters_ref, head_ref, lag_ref, last_ref, matrix_hbm,
    out_ref,
    traces_buf, spectra, matrix_buf, total, tail_ref, folded, partials, landed,
    trace_sem, own_sem, pair_send, pair_recv,
    right_send, right_recv, left_send, left_recv, out_send, out_recv,
):
    n, shots, receivers, length, freqs, taps, bin_count, rows = dims
    chips, half = n // 2, n // 4
    groups = freqs // GROUP
    width = GROUP * 2 * rows
    me = lax.axis_index("rows")
    chip, core = me // 2, me % 2
    place = jnp.where(chip % 2 == 0, chip // 2, chips - 1 - chip // 2)

    def chip_at(position):
        position = (position + 2 * chips) % chips
        return jnp.where(position < half, 2 * position, 2 * (chips - 1 - position) + 1)

    right = chip_at(place + 1) * 2 + core
    left = chip_at(place - 1) * 2 + core
    sibling = chip * 2 + 1 - core

    def trace_copy(shot):
        return pltpu.make_async_copy(traces_hbm.at[shot], traces_buf.at[shot], trace_sem.at[shot])

    for shot in range(shots):
        trace_copy(shot).start()

    barrier = pltpu.get_barrier_semaphore()
    for step in range(1, n):
        pl.semaphore_signal(
            barrier, inc=1, device_id={"rows": (me + step) % n}, device_id_type=MESH
        )

    def columns(block, side):
        return pl.ds(pl.multiple_of((block * 2 + side) * receivers, receivers), receivers)

    def own_copy(block):
        return pltpu.make_async_copy(
            matrix_hbm.at[:, :, :, columns(block, core)],
            matrix_buf.at[block, core],
            own_sem.at[block],
        )

    def pair_copy(block):
        return pltpu.make_async_remote_copy(
            src_ref=matrix_hbm.at[:, :, :, columns(block, 1 - core)],
            dst_ref=matrix_buf.at[block, core],
            send_sem=pair_send.at[block],
            recv_sem=pair_recv.at[block],
            device_id={"rows": sibling},
            device_id_type=MESH,
        )

    def ring_copy(step, shot, rightward):
        block = chip_at(place - (step - 1)) if rightward else chip_at(place + (step - 1))
        send, recv = (right_send, right_recv) if rightward else (left_send, left_recv)
        return pltpu.make_async_remote_copy(
            src_ref=spectra.at[block, shot],
            dst_ref=spectra.at[block, shot],
            send_sem=send.at[step - 1, shot],
            recv_sem=recv.at[step - 1, shot],
            device_id={"rows": right if rightward else left},
            device_id_type=MESH,
        )

    def arrival(step, shot, rightward):
        block = chip_at(place - step) if rightward else chip_at(place + step)
        send, recv = (right_send, right_recv) if rightward else (left_send, left_recv)
        return pltpu.make_async_remote_copy(
            src_ref=spectra.at[block, shot],
            dst_ref=spectra.at[block, shot],
            send_sem=send.at[step - 1, shot],
            recv_sem=recv.at[step - 1, shot],
            device_id={"rows": right if rightward else left},
            device_id_type=MESH,
        )

    def reach(shot, rightward):
        return half if (shot % 2 == 0) == rightward else half - 1

    highest = lax.Precision.HIGHEST
    contract = (((1,), (1,)), ((), ()))
    gains = lax.dot_general(
        lag_ref[...], filters_ref[...], contract, precision=highest,
        preferred_element_type=jnp.float32,
    )
    taps_cube = (bin_count, taps, taps)
    delay = sum(lax.broadcasted_iota(jnp.int32, taps_cube, axis) for axis in (1, 2))
    kept = jnp.where(
        delay < taps, jnp.broadcast_to(filters_ref[...][:, None, :], taps_cube), 0.0
    )
    cut = lax.dot_general(
        lag_ref[...], kept.reshape(bin_count * taps, taps), contract, precision=highest,
        preferred_element_type=jnp.float32,
    )
    cut_re, cut_im = cut[:freqs], cut[freqs:]
    last_re, last_im = last_ref[0], last_ref[1]
    tail_ref[:freqs] = (cut_re * last_re - cut_im * last_im).astype(jnp.bfloat16)
    tail_ref[freqs:] = (cut_re * last_im + cut_im * last_re).astype(jnp.bfloat16)
    bin_index = lax.broadcasted_iota(jnp.int32, (bin_count, receivers), 0)

    for shot in range(shots):
        trace_copy(shot).wait()
        chosen = bins_ref[shot : shot + 1, :]
        transform = lax.dot_general(
            head_ref[...], traces_buf[shot], contract, preferred_element_type=jnp.float32
        )
        onehot = (bin_index == chosen).astype(jnp.float32)
        gain = lax.dot_general(
            gains, onehot, (((1,), (0,)), ((), ())), precision=highest,
            preferred_element_type=jnp.float32,
        )
        ending = traces_buf[shot, :, length - 128 :].astype(jnp.float32).T[128 - taps :]
        masked = jnp.concatenate(
            [jnp.where(chosen == b, ending, 0.0) for b in range(bin_count)], axis=0
        ).astype(jnp.bfloat16)
        tail = jnp.dot(tail_ref[...], masked, preferred_element_type=jnp.float32)
        re, im = transform[:freqs], transform[freqs:]
        gain_re, gain_im = gain[:freqs], gain[freqs:]
        spectra[chip, shot, 0] = (re * gain_re - im * gain_im + tail[:freqs]).astype(jnp.bfloat16)
        spectra[chip, shot, 1] = (re * gain_im + im * gain_re + tail[freqs:]).astype(jnp.bfloat16)
        if shot == 0:
            pl.semaphore_wait(barrier, n - 1)
        for rightward in (True, False):
            ring_copy(1, shot, rightward).start()
        if shot == 0:
            for block in range(chips):
                own_copy(block).start()
                pair_copy(block).start()

    def multiply(block, first=False):
        for group in range(groups):
            signal = spectra[block, :, :, group * GROUP : (group + 1) * GROUP, :]
            matrix = matrix_buf[block, :, group * GROUP : (group + 1) * GROUP]
            product = lax.dot_general(
                signal.reshape(shots * 2 * GROUP, receivers),
                matrix.reshape(2 * width, receivers),
                contract,
                preferred_element_type=jnp.float32,
            )
            total[group] = product if first else total[group] + product

    for step in range(1, half + 1):
        for shot in range(shots):
            for rightward in (True, False):
                limit = reach(shot, rightward)
                if step <= limit:
                    arrival(step, shot, rightward).wait_recv()
                if step + 1 <= limit:
                    ring_copy(step + 1, shot, rightward).start()
        if step == 1:
            for block in range(chips):
                own_copy(block).wait()
                pair_copy(block).wait_recv()
            multiply(chip, True)
        multiply(chip_at(place - step))
        if step < half:
            multiply(chip_at(place + step))

    lane = lax.broadcasted_iota(jnp.int32, (GROUP, 2 * width), 1)
    diagonal = (lane % width) // (2 * rows) == lax.broadcasted_iota(
        jnp.int32, (GROUP, 2 * width), 0
    )
    for group in range(groups):
        for shot in range(shots):
            for part in range(2):
                start = (shot * 2 + part) * GROUP
                piece = jnp.where(diagonal, total[group, start : start + GROUP, :], 0.0)
                folded[part, shot : shot + 1, :] = jnp.sum(piece, axis=0, keepdims=True)
        straight, crossed = folded[0], folded[1]
        side = lax.broadcasted_iota(jnp.int32, (shots, 2 * width), 1) // rows % 2
        ahead = pltpu.roll(crossed, 2 * width - rows, 1)
        behind = pltpu.roll(crossed, rows, 1)
        partials[group] = jnp.where(side == 0, straight - ahead, straight + behind)

    share = freqs // n

    def out_copy(step):
        target = (me + step) % n
        return pltpu.make_async_remote_copy(
            src_ref=partials.at[target * share // GROUP],
            dst_ref=landed.at[me],
            send_sem=out_send.at[step - 1],
            recv_sem=out_recv.at[step - 1],
            device_id={"rows": target},
            device_id_type=MESH,
        )

    def out_arrival(step):
        source = (me + n - step) % n
        return pltpu.make_async_remote_copy(
            src_ref=partials.at[0],
            dst_ref=landed.at[source],
            send_sem=out_send.at[step - 1],
            recv_sem=out_recv.at[step - 1],
            device_id={"rows": source},
            device_id_type=MESH,
        )

    for step in range(1, n):
        out_copy(step).start()
    landed[me] = partials[me * share // GROUP]
    for step in range(1, n):
        out_arrival(step).wait_recv()
    for block in range(chips):
        out_ref[block] = landed[2 * block] + landed[2 * block + 1]

    for step in range(1, half + 1):
        for shot in range(shots):
            for rightward in (True, False):
                if step <= reach(shot, rightward):
                    ring_copy(step, shot, rightward).wait_send()
    for block in range(chips):
        pair_copy(block).wait_send()
    for step in range(1, n):
        out_copy(step).wait_send()


def fused(n, traces, offset_bin, filters, data_matrix):
    shots, receivers, length = traces.shape
    freqs, _, rows, positions = data_matrix.shape
    bin_count, taps = filters.shape
    chips, half, groups, width = n // 2, n // 4, freqs // GROUP, GROUP * 2 * rows
    head, lag, last = constants(freqs, length, taps, bin_count)
    dims = (n, shots, receivers, length, freqs, taps, bin_count, rows)
    vmem = pl.BlockSpec(memory_space=pltpu.VMEM)
    hbm = pl.BlockSpec(memory_space=pl.ANY)
    dma = pltpu.SemaphoreType.DMA
    landed = pl.pallas_call(
        functools.partial(fused_kernel, dims),
        out_shape=jax.ShapeDtypeStruct((chips, shots, 2 * width), jnp.float32),
        in_specs=[hbm, vmem, vmem, vmem, vmem, vmem, hbm],
        out_specs=vmem,
        scratch_shapes=[
            pltpu.VMEM((shots, receivers, length), jnp.bfloat16),
            pltpu.VMEM((chips, shots, 2, freqs, receivers), jnp.bfloat16),
            pltpu.VMEM((chips, 2, freqs, 2, rows, receivers), jnp.bfloat16),
            pltpu.VMEM((groups, shots * 2 * GROUP, 2 * width), jnp.float32),
            pltpu.VMEM((2 * freqs, bin_count * taps), jnp.bfloat16),
            pltpu.VMEM((2, shots, 2 * width), jnp.float32),
            pltpu.VMEM((groups, shots, 2 * width), jnp.float32),
            pltpu.VMEM((n, shots, 2 * width), jnp.float32),
            dma((shots,)), dma((chips,)), dma((chips,)), dma((chips,)),
            dma((half, shots)), dma((half, shots)), dma((half, shots)), dma((half, shots)),
            dma((n - 1,)), dma((n - 1,)),
        ],
        compiler_params=pltpu.CompilerParams(
            collective_id=0, has_side_effects=True, vmem_limit_bytes=60 * 1024 * 1024
        ),
    )(traces, offset_bin, filters, head, lag, last, data_matrix)
    share = freqs // n
    me = lax.axis_index("rows")
    split = landed.reshape(chips, shots, 2, GROUP, 2, rows)
    mine = lax.dynamic_slice_in_dim(split, me * share % GROUP, share, axis=3)
    ordered = mine.transpose(3, 4, 1, 0, 2, 5)
    return ordered.reshape(share, 2, shots, n * rows).astype(jnp.bfloat16)


def shards(n, traces, offset_bin, filters, data_matrix):
    freqs, _, rows, _ = data_matrix.shape
    share = freqs // n
    fits = (
        n % 4 == 0 and traces.shape[1] % 128 == 0 and traces.shape[2] % 128 == 0
        and freqs % GROUP == 0 and share > 0 and GROUP % share == 0
        and GROUP * 2 * rows % 128 == 0 and filters.shape[1] <= 128
    )
    if fits:
        return fused(n, traces, offset_bin, filters, data_matrix)
    return plain(traces, offset_bin, filters, data_matrix)


def solution(mesh):
    in_specs = (P("parts", "rows", None), P("parts", "rows"), P(), P("parts", None, "rows", None))
    out_specs = P(("parts", "rows"), None, None, None)
    body = functools.partial(shards, mesh.shape["rows"])
    return jax.shard_map(body, mesh=mesh, in_specs=in_specs, out_specs=out_specs, check_vma=False)
```

```python
import functools
import math

import jax
import jax.numpy as jnp
import ml_dtypes
import numpy as np
from jax import lax
from jax.experimental import pallas as pl
from jax.experimental.pallas import tpu as pltpu
from jax.sharding import PartitionSpec as P

FIRST = 64
GROUP = 16
MESH = pl.DeviceIdType.MESH


def spectral_table(freq_count, first_index, length):
    freq_index = first_index + jnp.arange(freq_count, dtype=jnp.int32)
    sample_index = jnp.arange(length, dtype=jnp.int32)
    product_index = freq_index[:, None] * sample_index[None, :] % length
    phase_angle = product_index.astype(jnp.float32) * jnp.float32(2.0 * math.pi / length)
    norm_factor = jnp.float32(1.0 / math.sqrt(length))
    stacked = jnp.stack([jnp.cos(phase_angle), -jnp.sin(phase_angle)], axis=1) * norm_factor
    return stacked.astype(jnp.bfloat16)


def condition(traces, offset_bin, filters):
    bin_count, tap_count = filters.shape
    length = traces.shape[2]
    selector = (
        offset_bin[:, :, None] == jnp.arange(bin_count, dtype=jnp.int32)[None, None, :]
    ).astype(jnp.float32)
    tap_rows = jnp.einsum("skb,bj->skj", selector, filters, precision=lax.Precision.HIGHEST)
    padded = jnp.pad(traces, ((0, 0), (0, 0), (tap_count - 1, 0)))
    filtered = jnp.zeros(traces.shape, jnp.float32)
    for delay_index in range(tap_count):
        window = padded[:, :, tap_count - 1 - delay_index : tap_count - 1 - delay_index + length]
        filtered = filtered + tap_rows[:, :, delay_index : delay_index + 1] * window.astype(
            jnp.float32
        )
    return filtered.astype(jnp.bfloat16)


def spectra_of(filtered, table):
    shot_count, receivers, length = filtered.shape
    flat_table = table.reshape(-1, length)
    flat_signal = filtered.reshape(shot_count * receivers, length)
    values = lax.dot_general(
        flat_table, flat_signal, (((1,), (1,)), ((), ())), preferred_element_type=jnp.float32
    )
    return values.astype(jnp.bfloat16).reshape(table.shape[0], 2, shot_count * receivers)


def predict(matrix_block, spectral_block):
    real_part = jnp.einsum(
        "tion,toun->tui",
        matrix_block[:, 0],
        spectral_block[:, 0],
        preferred_element_type=jnp.float32,
    ) - jnp.einsum(
        "tion,toun->tui",
        matrix_block[:, 1],
        spectral_block[:, 1],
        preferred_element_type=jnp.float32,
    )
    imag_part = jnp.einsum(
        "tion,toun->tui",
        matrix_block[:, 0],
        spectral_block[:, 1],
        preferred_element_type=jnp.float32,
    ) + jnp.einsum(
        "tion,toun->tui",
        matrix_block[:, 1],
        spectral_block[:, 0],
        preferred_element_type=jnp.float32,
    )
    return jnp.stack([real_part, imag_part], axis=1)


def plain(traces, offset_bin, filters, data_matrix):
    shot_count, receivers, length = traces.shape
    freq_count = data_matrix.shape[0]
    row_count = data_matrix.shape[2]
    table = spectral_table(freq_count, FIRST, length)
    spectra = spectra_of(condition(traces, offset_bin, filters), table)
    tile_width = shot_count * receivers
    gathered = lax.all_gather(spectra, "rows", axis=2, tiled=True)
    groups = gathered.shape[2] // tile_width
    matrix_block = data_matrix.reshape(freq_count, 2, row_count, groups, receivers)
    spectral_block = gathered.reshape(freq_count, 2, groups, shot_count, receivers)
    partial_value = predict(matrix_block, spectral_block)
    return lax.all_to_all(
        partial_value.astype(jnp.bfloat16), "rows", split_axis=0, concat_axis=3, tiled=True
    )


def phases(index, length):
    angle = (index % length).astype(np.float64) * (2.0 * math.pi / length)
    return np.cos(angle), -np.sin(angle)


def constants(freq_count, length, taps, bins):
    freq = FIRST + np.arange(freq_count, dtype=np.int64)
    norm = 1.0 / math.sqrt(length)
    head = np.stack(phases(freq[:, None] * np.arange(length)[None], length)) * norm
    head[:, :, length - taps :] = 0.0
    head = head.reshape(2 * freq_count, length).astype(np.float32).astype(ml_dtypes.bfloat16)
    lag = np.stack(phases(freq[:, None] * np.arange(taps)[None], length))
    lag = lag.reshape(2 * freq_count, taps).astype(np.float32)
    last = np.stack(phases(freq[:, None] * (length - taps + np.arange(taps))[None], length)) * norm
    last = np.tile(last, (1, 1, bins)).astype(np.float32)
    return head, lag, last


def fused_kernel(
    dims, traces_hbm, bins_ref, filters_ref, head_ref, lag_ref, last_ref, matrix_hbm,
    out_ref,
    traces_buf, spectra, matrix_buf, total, tail_ref, folded, partials, landed,
    trace_sem, own_sem, pair_send, pair_recv,
    right_send, right_recv, left_send, left_recv, out_send, out_recv,
):
    n, shots, receivers, length, freqs, taps, bin_count, rows = dims
    chips, half = n // 2, n // 4
    groups = freqs // GROUP
    width = GROUP * 2 * rows
    me = lax.axis_index("rows")
    chip, core = me // 2, me % 2
    place = jnp.where(chip % 2 == 0, chip // 2, chips - 1 - chip // 2)

    def chip_at(position):
        position = (position + 2 * chips) % chips
        return jnp.where(position < half, 2 * position, 2 * (chips - 1 - position) + 1)

    right = chip_at(place + 1) * 2 + core
    left = chip_at(place - 1) * 2 + core
    sibling = chip * 2 + 1 - core

    def trace_copy(shot):
        return pltpu.make_async_copy(traces_hbm.at[shot], traces_buf.at[shot], trace_sem.at[shot])

    for shot in range(shots):
        trace_copy(shot).start()

    barrier = pltpu.get_barrier_semaphore()
    for step in range(1, n):
        pl.semaphore_signal(
            barrier, inc=1, device_id={"rows": (me + step) % n}, device_id_type=MESH
        )

    def columns(block, side):
        return pl.ds(pl.multiple_of((block * 2 + side) * receivers, receivers), receivers)

    def own_copy(block):
        return pltpu.make_async_copy(
            matrix_hbm.at[:, :, :, columns(block, core)],
            matrix_buf.at[block, core],
            own_sem.at[block],
        )

    def pair_copy(block):
        return pltpu.make_async_remote_copy(
            src_ref=matrix_hbm.at[:, :, :, columns(block, 1 - core)],
            dst_ref=matrix_buf.at[block, core],
            send_sem=pair_send.at[block],
            recv_sem=pair_recv.at[block],
            device_id={"rows": sibling},
            device_id_type=MESH,
        )

    def ring_copy(step, shot, rightward):
        block = chip_at(place - (step - 1)) if rightward else chip_at(place + (step - 1))
        send, recv = (right_send, right_recv) if rightward else (left_send, left_recv)
        return pltpu.make_async_remote_copy(
            src_ref=spectra.at[block, shot],
            dst_ref=spectra.at[block, shot],
            send_sem=send.at[step - 1, shot],
            recv_sem=recv.at[step - 1, shot],
            device_id={"rows": right if rightward else left},
            device_id_type=MESH,
        )

    def arrival(step, shot, rightward):
        block = chip_at(place - step) if rightward else chip_at(place + step)
        send, recv = (right_send, right_recv) if rightward else (left_send, left_recv)
        return pltpu.make_async_remote_copy(
            src_ref=spectra.at[block, shot],
            dst_ref=spectra.at[block, shot],
            send_sem=send.at[step - 1, shot],
            recv_sem=recv.at[step - 1, shot],
            device_id={"rows": right if rightward else left},
            device_id_type=MESH,
        )

    def reach(shot, rightward):
        return half if (shot % 2 == 0) == rightward else half - 1

    highest = lax.Precision.HIGHEST
    contract = (((1,), (1,)), ((), ()))
    gains = lax.dot_general(
        lag_ref[...], filters_ref[...], contract, precision=highest,
        preferred_element_type=jnp.float32,
    )
    taps_cube = (bin_count, taps, taps)
    delay = sum(lax.broadcasted_iota(jnp.int32, taps_cube, axis) for axis in (1, 2))
    kept = jnp.where(
        delay < taps, jnp.broadcast_to(filters_ref[...][:, None, :], taps_cube), 0.0
    )
    cut = lax.dot_general(
        lag_ref[...], kept.reshape(bin_count * taps, taps), contract, precision=highest,
        preferred_element_type=jnp.float32,
    )
    cut_re, cut_im = cut[:freqs], cut[freqs:]
    last_re, last_im = last_ref[0], last_ref[1]
    tail_ref[:freqs] = (cut_re * last_re - cut_im * last_im).astype(jnp.bfloat16)
    tail_ref[freqs:] = (cut_re * last_im + cut_im * last_re).astype(jnp.bfloat16)
    bin_index = lax.broadcasted_iota(jnp.int32, (bin_count, receivers), 0)

    for shot in range(shots):
        trace_copy(shot).wait()
        chosen = bins_ref[shot : shot + 1, :]
        transform = lax.dot_general(
            head_ref[...], traces_buf[shot], contract, preferred_element_type=jnp.float32
        )
        onehot = (bin_index == chosen).astype(jnp.float32)
        gain = lax.dot_general(
            gains, onehot, (((1,), (0,)), ((), ())), precision=highest,
            preferred_element_type=jnp.float32,
        )
        ending = traces_buf[shot, :, length - 128 :].astype(jnp.float32).T[128 - taps :]
        masked = jnp.concatenate(
            [jnp.where(chosen == b, ending, 0.0) for b in range(bin_count)], axis=0
        ).astype(jnp.bfloat16)
        tail = jnp.dot(tail_ref[...], masked, preferred_element_type=jnp.float32)
        re, im = transform[:freqs], transform[freqs:]
        gain_re, gain_im = gain[:freqs], gain[freqs:]
        spectra[chip, shot, 0] = (re * gain_re - im * gain_im + tail[:freqs]).astype(jnp.bfloat16)
        spectra[chip, shot, 1] = (re * gain_im + im * gain_re + tail[freqs:]).astype(jnp.bfloat16)
        if shot == 0:
            pl.semaphore_wait(barrier, n - 1)
        for rightward in (True, False):
            ring_copy(1, shot, rightward).start()
        if shot == 0:
            for block in range(chips):
                own_copy(block).start()
                pair_copy(block).start()

    def multiply(block, first=False):
        for group in range(groups):
            signal = spectra[block, :, :, group * GROUP : (group + 1) * GROUP, :]
            matrix = matrix_buf[block, :, group * GROUP : (group + 1) * GROUP]
            product = lax.dot_general(
                signal.reshape(shots * 2 * GROUP, receivers),
                matrix.reshape(2 * width, receivers),
                contract,
                preferred_element_type=jnp.float32,
            )
            total[group] = product if first else total[group] + product

    for step in range(1, half + 1):
        for shot in range(shots):
            for rightward in (True, False):
                limit = reach(shot, rightward)
                if step <= limit:
                    arrival(step, shot, rightward).wait_recv()
                if step + 1 <= limit:
                    ring_copy(step + 1, shot, rightward).start()
        if step == 1:
            for block in range(chips):
                own_copy(block).wait()
                pair_copy(block).wait_recv()
            multiply(chip, True)
        multiply(chip_at(place - step))
        if step < half:
            multiply(chip_at(place + step))

    lane = lax.broadcasted_iota(jnp.int32, (GROUP, 2 * width), 1)
    diagonal = (lane % width) // (2 * rows) == lax.broadcasted_iota(
        jnp.int32, (GROUP, 2 * width), 0
    )
    share = freqs // n
    span = 2 * rows * share
    for group in range(groups):
        for shot in range(shots):
            for part in range(2):
                start = (shot * 2 + part) * GROUP
                piece = jnp.where(diagonal, total[group, start : start + GROUP, :], 0.0)
                folded[part, shot : shot + 1, :] = jnp.sum(piece, axis=0, keepdims=True)
        straight, crossed = folded[0], folded[1]
        side = lax.broadcasted_iota(jnp.int32, (shots, 2 * width), 1) // rows % 2
        ahead = pltpu.roll(crossed, 2 * width - rows, 1)
        behind = pltpu.roll(crossed, rows, 1)
        result = jnp.where(side == 0, straight - ahead, straight + behind)
        for window in range(GROUP // share):
            start = 2 * width - window * span
            partials[group * (GROUP // share) + window] = jnp.where(
                lax.broadcasted_iota(jnp.int32, (shots, width), 1) < span,
                pltpu.roll(result[:, :width], start % width, 1),
                pltpu.roll(result[:, width:], (start + span) % width, 1),
            )

    def out_copy(step):
        target = (me + step) % n
        return pltpu.make_async_remote_copy(
            src_ref=partials.at[target],
            dst_ref=landed.at[me],
            send_sem=out_send.at[step - 1],
            recv_sem=out_recv.at[step - 1],
            device_id={"rows": target},
            device_id_type=MESH,
        )

    def out_arrival(step):
        source = (me + n - step) % n
        return pltpu.make_async_remote_copy(
            src_ref=partials.at[0],
            dst_ref=landed.at[source],
            send_sem=out_send.at[step - 1],
            recv_sem=out_recv.at[step - 1],
            device_id={"rows": source},
            device_id_type=MESH,
        )

    for step in sorted(range(1, n), key=lambda step: abs(step - n // 2)):
        out_copy(step).start()
    landed[me] = partials[me]
    for step in range(1, n):
        out_arrival(step).wait_recv()
    for block in range(chips):
        summed = landed[2 * block] + landed[2 * block + 1]
        out_ref[:, 2 * block, :] = summed[:, :span]
        out_ref[:, 2 * block + 1, :] = summed[:, span : 2 * span]

    for step in range(1, half + 1):
        for shot in range(shots):
            for rightward in (True, False):
                if step <= reach(shot, rightward):
                    ring_copy(step, shot, rightward).wait_send()
    for block in range(chips):
        pair_copy(block).wait_send()
    for step in range(1, n):
        out_copy(step).wait_send()


def fused(n, traces, offset_bin, filters, data_matrix):
    shots, receivers, length = traces.shape
    freqs, _, rows, _ = data_matrix.shape
    share = freqs // n
    bin_count, taps = filters.shape
    chips, half, groups, width = n // 2, n // 4, freqs // GROUP, GROUP * 2 * rows
    head, lag, last = constants(freqs, length, taps, bin_count)
    dims = (n, shots, receivers, length, freqs, taps, bin_count, rows)
    vmem = pl.BlockSpec(memory_space=pltpu.VMEM)
    hbm = pl.BlockSpec(memory_space=pl.ANY)
    dma = pltpu.SemaphoreType.DMA
    landed = pl.pallas_call(
        functools.partial(fused_kernel, dims),
        out_shape=jax.ShapeDtypeStruct((shots, n, 2 * rows * share), jnp.float32),
        in_specs=[hbm, vmem, vmem, vmem, vmem, vmem, hbm],
        out_specs=vmem,
        scratch_shapes=[
            pltpu.VMEM((shots, receivers, length), jnp.bfloat16),
            pltpu.VMEM((chips, shots, 2, freqs, receivers), jnp.bfloat16),
            pltpu.VMEM((chips, 2, freqs, 2, rows, receivers), jnp.bfloat16),
            pltpu.VMEM((groups, shots * 2 * GROUP, 2 * width), jnp.float32),
            pltpu.VMEM((2 * freqs, bin_count * taps), jnp.bfloat16),
            pltpu.VMEM((2, shots, 2 * width), jnp.float32),
            pltpu.VMEM((n, shots, width), jnp.float32),
            pltpu.VMEM((n, shots, width), jnp.float32),
            dma((shots,)), dma((chips,)), dma((chips,)), dma((chips,)),
            dma((half, shots)), dma((half, shots)), dma((half, shots)), dma((half, shots)),
            dma((n - 1,)), dma((n - 1,)),
        ],
        compiler_params=pltpu.CompilerParams(
            collective_id=0, has_side_effects=True, vmem_limit_bytes=60 * 1024 * 1024
        ),
    )(traces, offset_bin, filters, head, lag, last, data_matrix)
    ordered = landed.astype(jnp.bfloat16).reshape(shots, n, share, 2, rows)
    return ordered.transpose(2, 3, 0, 1, 4).reshape(share, 2, shots, n * rows)


def shards(n, traces, offset_bin, filters, data_matrix):
    freqs, _, rows, _ = data_matrix.shape
    share = freqs // n
    fits = (
        n % 4 == 0 and traces.shape[1] % 128 == 0 and traces.shape[2] % 128 == 0
        and freqs % GROUP == 0 and share > 0 and GROUP % (2 * share) == 0
        and GROUP * 2 * rows % 128 == 0 and filters.shape[1] <= 128
    )
    if fits:
        return fused(n, traces, offset_bin, filters, data_matrix)
    return plain(traces, offset_bin, filters, data_matrix)


def solution(mesh):
    in_specs = (P("parts", "rows", None), P("parts", "rows"), P(), P("parts", None, "rows", None))
    out_specs = P(("parts", "rows"), None, None, None)
    body = functools.partial(shards, mesh.shape["rows"])
    return jax.shard_map(body, mesh=mesh, in_specs=in_specs, out_specs=out_specs, check_vma=False)
```
